32 devices in a mesh: dp: 2 (over x), ctx: 16 (over z, y, core).
Axes of the slice: x: 2, y: 2, z: 4, core: 2. Of those that a mesh axis runs over, the one named last changes fastest.
Arguments:
- query_act: bfloat16 [2, 2048, 2048], P('dp', 'ctx'), may hold values from -6 to 6
- key_act: bfloat16 [2, 2048, 2048], P('dp', 'ctx'), may hold values from -6 to 6
- value_act: bfloat16 [2, 2048, 2048], P('dp', 'ctx'), may hold values from -6 to 6
- grad_out: bfloat16 [2, 2048, 2048], P('dp', 'ctx'), may hold values from -6 to 6
- filter_taps: bfloat16 [128, 2048], replicated, may hold values from -2.5 to 2.5
Outputs:
- output_act: bfloat16 [2, 2048, 2048], P('dp', 'ctx')
- grad_query: bfloat16 [2, 2048, 2048], P('dp', 'ctx')
- grad_key: bfloat16 [2, 2048, 2048], P('dp', 'ctx')
- grad_value: bfloat16 [2, 2048, 2048], P('dp', 'ctx')
- grad_filter: float32 [128, 2048], P(None, 'ctx')
The draws below stay inside these ranges and needn't reach their ends.
All inputs are finite; a program needn't handle non-finite values.
Results may differ from the reference program's by a relative error of at most 0.0065.
Values may be sent and summed in bfloat16 or wider, within the bound.
No kernel may reach another device: no remote copies, remote signals or barrier semaphores. Data moves between devices by JAX's collectives and lax.ppermute only.
A program may use at most 64 MiB of HBM per device.

```python
import math
import jax
import jax.numpy as jnp
from jax import lax

C = 2048
LH = 128
SEQS = 2
LEN = 2048


def draw_filter_taps(key, part):
    key = jax.random.fold_in(key, 7)
    rate_key, noise_key = jax.random.split(key, 2)
    horizon = jnp.exp(jax.random.uniform(rate_key, (C,), jnp.float32, math.log(8.0), math.log(600.0)))
    rough_part = jnp.clip(jax.random.normal(noise_key, (LH, C), jnp.float32), -4.0, 4.0)
    tap_index = jnp.arange(LH, dtype=jnp.float32)[:, None]
    falloff = jnp.exp(-tap_index / horizon[None, :])
    amplitude = 1.5 / jnp.sqrt(jnp.minimum(float(LH), horizon / 2.0) + 1.0)
    return jnp.clip(rough_part * falloff * amplitude[None, :], -2.5, 2.5).astype(jnp.bfloat16)


def raised(entries, stream_key, source, target, parts, factor):
    def block_of(position):
        return (jnp.arange(entries.shape[position]) // (entries.shape[position] // parts)).reshape((-1,) + (1,) * (entries.ndim - 1 - position))

    first = jax.random.permutation(stream_key, parts)[block_of(target)]
    second = (block_of(target) + parts // 2) % parts
    return jnp.where((block_of(source) == first) | (block_of(source) == second), factor * entries, entries)


def block_levels(key, dims, cuts, least, top_value):
    gain, own = 1.0, jax.random.fold_in(key, 6)
    for axis_at, parts in cuts:
        draws = jnp.exp(jax.random.uniform(jax.random.fold_in(own, axis_at), (parts,), jnp.float32, least / len(cuts), top_value / len(cuts)))
        gain = gain * jnp.repeat(draws, dims[axis_at] // parts).reshape([-1 if axis == axis_at else 1 for axis in range(len(dims))])
    return gain


def bell_draw(key, extent, width, limit, pieces=(), held_as=jnp.bfloat16):
    values = width * jax.random.normal(key, extent, jnp.float32)
    if pieces:
        values = values * block_levels(key, extent, pieces, -0.22, 0.18)
    return jnp.clip(values, -limit, limit).astype(held_as)


def heavy_noise(stream_key, extent, deviation, reach, cuts, heavy, held_as=jnp.bfloat16):
    values = deviation * jax.random.normal(stream_key, extent, jnp.float32)
    if cuts:
        values = values * block_levels(stream_key, extent, cuts, -0.22, 0.18)
    return jnp.clip(raised(values, jax.random.fold_in(stream_key, 3), *heavy), -reach, reach).astype(held_as)


def setup_inputs(seed: int = 0) -> dict:
    keys = jax.random.split(jax.random.key(seed), 6)
    query_act = bell_draw(keys[0], (SEQS, LEN, C), 1.0, 6.0, ((0, 2), (1, 16)))
    key_act = bell_draw(keys[1], (SEQS, LEN, C), 1.0, 6.0, ((0, 2), (1, 16)))
    value_act = bell_draw(keys[2], (SEQS, LEN, C), 1.0, 6.0, ((0, 2), (1, 16)))
    grad_out = heavy_noise(keys[3], (SEQS, LEN, C), 1.0, 6.0, ((0, 2), (1, 16)), (1, 2, 16, 2.0))
    filter_taps = draw_filter_taps(jax.random.fold_in(keys[5], 71), 0)
    return dict(query_act=query_act, key_act=key_act, value_act=value_act, grad_out=grad_out, filter_taps=filter_taps)


def fft_conv(first_arr, second_arr, size_fft):
    spectrum = jnp.fft.rfft(first_arr, size_fft, axis=0) * jnp.fft.rfft(second_arr, size_fft, axis=0)
    return jnp.fft.irfft(spectrum, size_fft, axis=0)

def reference(query_act, key_act, value_act, grad_out, filter_taps):
    weights = filter_taps.astype(jnp.float32)
    size_fft = 2 * LEN

    def one_sequence(items):
        query_rows, key_rows, value_rows, grad_rows = items
        query_f = query_rows.astype(jnp.float32)
        key_f = key_rows.astype(jnp.float32)
        value_f = value_rows.astype(jnp.float32)
        grad_f = grad_rows.astype(jnp.float32)
        kv_product = (key_f * value_f).astype(jnp.bfloat16).astype(jnp.float32)
        filtered = fft_conv(kv_product, weights, size_fft)[:LEN]
        output_rows = (query_f * filtered).astype(jnp.bfloat16)
        grad_query_rows = (grad_f * filtered).astype(jnp.bfloat16)
        gate_grad = (grad_f * query_f).astype(jnp.bfloat16).astype(jnp.float32)
        reversed_grad = gate_grad[::-1]
        flowing = fft_conv(reversed_grad, weights, size_fft)[:LEN][::-1]
        grad_key_rows = (flowing * value_f).astype(jnp.bfloat16)
        grad_value_rows = (flowing * key_f).astype(jnp.bfloat16)
        crossed = fft_conv(reversed_grad, kv_product, size_fft)
        lagged = crossed[LEN - LH:LEN][::-1]
        return (output_rows, grad_query_rows, grad_key_rows, grad_value_rows, lagged)
    outputs = lax.map(one_sequence, (query_act, key_act, value_act, grad_out))
    grad_filter = lax.optimization_barrier(jnp.sum(outputs[4], axis=0)) * (1.0 / math.sqrt(SEQS * LEN))
    return (outputs[0], outputs[1], outputs[2], outputs[3], grad_filter)
```

```python
import functools
import math

import jax
import jax.numpy as jnp
import ml_dtypes
import numpy as np
from jax import lax
from jax.experimental import pallas as pl
from jax.experimental.pallas import tpu as pltpu
from jax.sharding import PartitionSpec as P

bf16 = jnp.bfloat16
f32 = jnp.float32
small_bytes = 10 * 1024 * 1024
large_bytes = 20 * 1024 * 1024
pieces_inside = 4
tile = 512
lanes = 128
load_rows = 32
near = pl.BlockSpec(memory_space=pltpu.VMEM)
far = pl.BlockSpec(memory_space=pltpu.HBM)


def high_low(matrix):
    high = matrix.astype(ml_dtypes.bfloat16)
    low = (matrix - high.astype(np.float64)).astype(ml_dtypes.bfloat16)
    return high, low


def transforms(size, taps):
    angle = np.pi * (4 * np.arange(size) + 1) / (2 * size)
    phase = angle[:, None] * np.arange(size)[None, :]
    real, imag = np.cos(phase), np.sin(phase)
    one = np.concatenate([real, imag], axis=0)
    upper = np.concatenate([-imag.T, real.T], axis=1) / size
    lower = np.concatenate([real.T, imag.T], axis=1) / size
    lag = (size - np.arange(taps))[:, None] * angle[None, :]
    lags = np.concatenate([np.cos(lag), np.sin(lag)], axis=1) / size
    turned = np.concatenate([imag.T, -real.T], axis=1)[:taps] / size

    def forward(matrix):
        return np.concatenate(high_low(matrix), axis=1)

    def inverse(matrix):
        high, low = high_low(matrix)
        return np.concatenate([high, high, low], axis=1)

    return (
        forward(one[:, :taps]),
        forward(one),
        inverse(upper),
        inverse(lower),
        np.stack([inverse(lags), inverse(turned)]),
    )


def spectrum(matrix, block):
    stacked = jnp.concatenate([block, block], axis=0)
    both = jnp.dot(matrix, stacked, preferred_element_type=f32)
    half = both.shape[0] // 2
    return both[:half], both[half:]


def back(matrix, real, imag):
    both = jnp.concatenate([real, imag], axis=0)
    high = both.astype(bf16)
    low = (both - high.astype(f32)).astype(bf16)
    return jnp.dot(
        matrix, jnp.concatenate([high, low, high], axis=0), preferred_element_type=f32
    )


def times(left, right):
    (lr, li), (rr, ri) = left, right
    return lr * rr - li * ri, lr * ri + li * rr


def times_conjugate(left, right):
    (lr, li), (rr, ri) = left, right
    return lr * rr + li * ri, li * rr - lr * ri


def window(first, second):
    return first[0] - second[1], first[1] + second[0]


def product(left, right):
    return (left.astype(f32) * right.astype(f32)).astype(bf16)


def forward_strip(one, upper, before, kv, weights, query, grad):
    both = window(spectrum(one, before), spectrum(one, kv))
    mixed = back(upper, *times(both, weights))
    return (query.astype(f32) * mixed).astype(bf16), (grad.astype(f32) * mixed).astype(bf16)


def backward_strip(one, lower, gate, beyond, weights, key, value):
    both = window(spectrum(one, gate), spectrum(one, beyond))
    flowing = back(lower, *times_conjugate(both, weights))
    return (flowing * value.astype(f32)).astype(bf16), (flowing * key.astype(f32)).astype(bf16)


def tiles(ref):
    return [slice(at, at + tile) for at in range(0, ref.shape[1], tile)]


def halves(ref):
    size = ref.shape[0] // 2
    return slice(0, size), slice(size, 2 * size)


def core():
    return lax.rem(lax.axis_index("ctx"), 2)


def blocks(parity, number, share):
    first = number * (tile // share)
    return [
        slice((2 * place + parity) * share, (2 * place + parity + 1) * share)
        for place in range(first, first + tile // share)
    ]


def gather(ref, columns):
    return jnp.concatenate([ref[:, cols] for cols in columns], axis=1)


def take(pieces, start, stop):
    width = pieces[0].shape[1]
    return jnp.concatenate(
        [
            pieces[at // width][:, at % width : at % width + lanes]
            for at in range(start, stop, lanes)
        ],
        axis=1,
    )


def wait(copies):
    for copy in copies:
        copy.wait()


def first_kernel(share, query, grad, key, value, out, left, right, sems):
    count = out.shape[1] // share

    def copies(pair, parity):
        return [
            pltpu.make_async_copy(
                source.at[:, (2 * place + parity) * share : (2 * place + parity + 1) * share],
                held.at[:, place * share : (place + 1) * share],
                sems.at[which, place],
            )
            for place in range(count)
            for which, (source, held) in enumerate(zip(pair, (left, right)))
        ]

    for parity, pair in enumerate(((query, grad), (key, value))):

        @pl.when(core() == parity)
        def _():
            for copy in copies(pair, 1 - parity):
                copy.start()

    for place, copy in enumerate(copies((key, value), 0)):
        copy.wait()
        if place % 2:
            cols = slice(place // 2 * share, (place // 2 + 1) * share)
            out[:, cols] = product(left[:, cols], right[:, cols])


def start_loads(sources, held, sems):
    rows = [slice(at, at + load_rows) for at in range(0, held[0].shape[0], load_rows)]
    groups = [
        [
            pltpu.make_async_copy(source.at[part], place.at[part], sems.at[which, number])
            for which, (source, place) in enumerate(zip(sources, held))
        ]
        for number, part in enumerate(rows)
    ]
    for group in groups:
        for copy in group:
            copy.start()
    return rows, groups


def prepare_kernel(share, *refs):
    sources, held, base, sends, sems = refs[:4], refs[5:9], refs[9], refs[10:-1], refs[-1]
    query, grad, key, value = held
    half, width = base.shape[1], sends[0].shape[1]
    rows, groups = start_loads(sources, held, sems)

    def run(parity):
        pairs = (key, value), (query, grad)
        first, second = pairs if parity == 0 else pairs[::-1]
        for part, group in zip(rows, groups):
            wait(group)
            for offset in range(0, half, lanes):
                start = 2 * (offset // share) * share + offset % share
                own = slice(start + parity * share, start + parity * share + lanes)
                other = slice(start + (1 - parity) * share, start + (1 - parity) * share + lanes)

                def put(ref, at, pair, cols):
                    ref[part, at : at + lanes] = product(pair[0][part, cols], pair[1][part, cols])

                put(base, offset, second, own)
                for number, (pair, cols) in enumerate(
                    ((second, other), (first, other), (first, own))
                ):
                    where = number * half + offset
                    put(sends[where // width], where % width, pair, cols)

    for parity in range(2):
        pl.when(core() == parity)(functools.partial(run, parity))


def inside_kernel(one, base, *refs):
    sends, came = refs[:pieces_inside], refs[pieces_inside : 2 * pieces_inside]
    cross, spectra = refs[2 * pieces_inside :]
    sign = 1.0 - 2.0 * core().astype(f32)
    real, imag = halves(cross)
    half = base.shape[1]
    for cols in tiles(base):
        low, high = cols.start, cols.stop
        own_first = spectrum(one[...], take(sends, 2 * half + low, 2 * half + high))
        own_base = spectrum(one[...], base[:, cols])
        other_first = spectrum(one[...], take(came, low, high))
        other_base = spectrum(one[...], take(came, half + low, half + high))
        spectra[real, cols], spectra[imag, cols] = own_base
        ar, ai = times_conjugate(own_first, own_base)
        both = own_first[0] - sign * other_first[1], own_first[1] + sign * other_first[0]
        br, bi = times_conjugate(both, other_base)
        cross[real, cols] = br - sign * ai
        cross[imag, cols] = bi + sign * ar


def divide(totals, sends, level):
    width, below, here = level
    own = lax.rem(lax.div(lax.axis_index("ctx"), 2 * here), width)
    for number, send in enumerate(sends):
        other = jnp.bitwise_xor(own, number)
        for place in range(below):
            send[place] = totals[other * below + place].astype(send.dtype)


def lag_kernel(level, one, lags, halo, cross, spectra, *refs):
    sends, totals = refs[:-1], refs[-1]
    real, imag = halves(cross)
    share = totals.shape[2]
    matrix = lags[core()]
    for cols in tiles(halo):
        ar, ai = times_conjugate(
            spectrum(one[...], halo[:, cols]), (spectra[real, cols], spectra[imag, cols])
        )
        sums = back(matrix, cross[real, cols] + ar, cross[imag, cols] + ai)
        for start in range(0, tile, share):
            totals[(cols.start + start) // share] = sums[:, start : start + share]
    divide(totals, sends, level)


def join_kernel(level, came, keep, *refs):
    arrived, sends, totals = refs[:came], refs[came + 1 : -1], refs[-1]
    for place in range(totals.shape[0]):
        value = keep[place]
        for part in arrived:
            value = value + part[place].astype(f32)
        totals[place] = value
    divide(totals, sends, level)


def total_kernel(scale, *refs):
    parts, (out, held, sem) = refs[:-4], refs[-3:]
    planes = []
    for plane in (parts[: len(parts) // 2], parts[len(parts) // 2 :]):
        value = plane[0][0].astype(f32)
        for part in plane[1:]:
            value = value + part[0].astype(f32)
        planes.append(value)
    held[...] = (planes[0] + planes[1]) * scale
    copy = pltpu.make_async_copy(held, out, sem)
    copy.start()
    copy.wait()


def spread(held, results, columns, share):
    for which, result in enumerate(results):
        for number, cols in enumerate(columns):
            held[which, :, cols] = result[:, number * share : (number + 1) * share]


def send_out(held, outs, cols, sems):
    copies = [
        pltpu.make_async_copy(held.at[which, :, cols], out.at[:, cols], sems.at[which])
        for which, out in enumerate(outs)
    ]
    for copy in copies:
        copy.start()
    return copies


def rows_of(array, count):
    size = array.shape[0] // count
    return [slice(at, at + size) for at in range(0, array.shape[0], size)]


def inside_way_kernel(share, query, key, value, grad, one, *refs):
    fetched, came, refs = refs[:3], refs[3 : 3 + pieces_inside], refs[4 + pieces_inside :]
    held, upper, lower, taps, sems = refs
    half = taps.shape[1] // 2
    fetches = [
        pltpu.make_async_copy(source.at[rows], place.at[rows], sems.at[number, part])
        for number, (source, place) in enumerate(zip(fetched, (upper, lower, taps)))
        for part, rows in enumerate(rows_of(place, sems.shape[1]))
    ]
    for fetch in fetches:
        fetch.start()
    wait(fetches)

    def run(parity):
        for number in range(half // tile):
            for side in (parity, 1 - parity):
                columns = blocks(side, number, share)
                start = (half if side == parity else 2 * half) + number * tile
                halo = take(came, start, start + tile)
                weights = spectrum(one[...], gather(taps, columns))
                around = gather(query, columns), gather(grad, columns)
                within = gather(key, columns), gather(value, columns)
                if parity == 0:
                    results = backward_strip(
                        one[...], lower[...], product(*around), halo, weights, *within
                    )
                else:
                    results = forward_strip(
                        one[...], upper[...], halo, product(*within), weights, *around
                    )
                spread(held, results, columns, share)

    for parity in range(2):
        pl.when(core() == parity)(functools.partial(run, parity))


def across_way(share, late, parity, held, query, key, value, grad, one, upper, lower, taps, halo):
    for number in range(halo.shape[1] // tile):
        packed = slice(number * tile, (number + 1) * tile)
        columns = blocks(1 - parity if late else parity, number, share)
        weights = spectrum(one[...], gather(taps, columns))
        around = gather(query, columns), gather(grad, columns)
        within = gather(key, columns), gather(value, columns)
        if parity == 0:
            results = forward_strip(
                one[...], upper[...], halo[:, packed], product(*within), weights, *around
            )
        else:
            results = backward_strip(
                one[...], lower[...], product(*around), halo[:, packed], weights, *within
            )
        spread(held, results, columns, share)
        yield columns


def across_first_kernel(share, *refs):
    inputs, before, refs = refs[:9], refs[9], refs[11:]
    outs, held, sems = refs[:4], refs[4], refs[5]

    def run(parity):
        inner = outs[2:] if parity == 0 else outs[:2]
        copies = [
            pltpu.make_async_copy(before.at[which, rows], out.at[rows], sems.at[which, part])
            for which, out in enumerate(inner)
            for part, rows in enumerate(rows_of(out, sems.shape[1]))
        ]
        for copy in copies:
            copy.start()
        for _ in across_way(share, False, parity, held, *inputs):
            pass
        wait(copies)

    for parity in range(2):
        pl.when(core() == parity)(functools.partial(run, parity))


def across_late_kernel(share, *refs):
    inputs, before, refs = refs[:9], refs[9], refs[15:]
    outs, held, sems = refs[:4], refs[4], refs[5]

    def run(parity):
        outer = outs[:2] if parity == 0 else outs[2:]
        copies = []
        for number in range(inputs[-1].shape[1] // tile):
            for which, cols in enumerate(blocks(parity, number, share)):
                place = sems.at[0, number * (tile // share) + which]
                copies += send_out(before, outer, cols, place)
        for number, columns in enumerate(across_way(share, True, parity, held, *inputs)):
            for which, cols in enumerate(columns):
                place = sems.at[1, number * len(columns) + which]
                copies += send_out(held, outer, cols, place)
        wait(copies)

    for parity in range(2):
        pl.when(core() == parity)(functools.partial(run, parity))


def plain_load_kernel(*refs):
    query, grad, key, value, kv, gate, sems = refs[4:]
    rows, groups = start_loads(refs[:4], refs[4:8], sems)
    for part, group in zip(rows, groups):
        wait(group)
        kv[part] = product(key[part], value[part])
        gate[part] = product(query[part], grad[part])


def plain_lag_kernel(one, lags, before, kv, gate, sums):
    for cols in tiles(kv):
        both = window(spectrum(one[...], before[:, cols]), spectrum(one[...], kv[:, cols]))
        values = back(lags[0], *times_conjugate(both, spectrum(one[...], gate[:, cols])))
        sums[:, cols] = values.astype(bf16)


def plain_filter_kernel(
    first, one, upper, lower, before, kv, gate, beyond, taps, query, key, value, grad,
    output, grad_query, grad_key, grad_value,
):
    for cols in tiles(kv):
        weights = spectrum(first[...], taps[:, cols])
        output[:, cols], grad_query[:, cols] = forward_strip(
            one[...], upper[...], before[:, cols], kv[:, cols], weights,
            query[:, cols], grad[:, cols],
        )
        grad_key[:, cols], grad_value[:, cols] = backward_strip(
            one[...], lower[...], gate[:, cols], beyond[:, cols], weights,
            key[:, cols], value[:, cols],
        )


def call(
    kernel, name, inputs, outs, scratch=(), far_ins=(), any_ins=(), far_outs=(),
    limit=small_bytes, flops=0, **more
):
    def space(at):
        return pl.ANY if at in any_ins else pltpu.HBM if at in far_ins else pltpu.VMEM

    inputs = [
        pltpu.with_memory_space_constraint(array, space(at)) for at, array in enumerate(inputs)
    ]
    return pl.pallas_call(
        kernel,
        in_specs=[pl.BlockSpec(memory_space=space(at)) for at in range(len(inputs))],
        out_specs=[far if at in far_outs else near for at in range(len(outs))],
        out_shape=[
            (pltpu.HBM if at in far_outs else pltpu.VMEM)(out.shape, out.dtype)
            for at, out in enumerate(outs)
        ],
        scratch_shapes=scratch,
        cost_estimate=pl.CostEstimate(flops=flops, bytes_accessed=0, transcendentals=0),
        compiler_params=pltpu.CompilerParams(vmem_limit_bytes=limit),
        name=name,
        **more,
    )(*inputs)


def shift(array, axis, by):
    devices = lax.axis_size(axis)
    return lax.ppermute(
        array, axis, [(i, i + by) for i in range(devices) if 0 <= i + by < devices]
    )


def sum_over_dp(own):
    dp = lax.axis_size("dp")
    if dp == 1:
        return own
    if dp == 2:
        return own + lax.ppermute(own, "dp", [(0, 1), (1, 0)])
    came = [own] + [
        lax.ppermute(own, "dp", [(i, (i + by) % dp) for i in range(dp)]) for by in range(1, dp)
    ]
    order = lax.rem(lax.axis_index("dp") - jnp.arange(dp) + dp, dp)
    return jnp.sum(jnp.stack(came)[order], axis=0)


def shape(dims, dtype):
    return jax.ShapeDtypeStruct(dims, dtype)


def levels(ctx):
    chips, found = ctx // 2, []
    while chips > 1:
        width = 4 if chips % 4 == 0 else 2
        chips //= width
        found.append((width, chips, chips))
    return found


def paired(query, key, value, grad, filter_taps):
    length, channels = query.shape
    taps = filter_taps.shape[0]
    ctx = lax.axis_size("ctx")
    share = channels // ctx
    half = channels // 2
    _, one, upper, lower, lags = transforms(length, taps)
    block, strip = shape((length, channels), bf16), shape((length, half), bf16)
    spectra = shape((2 * length, half), f32)
    sources = query, grad, key, value
    inside = [(i, i ^ 1) for i in range(ctx)]
    across = [(i, i + 1) for i in range(1, ctx - 1, 2)]
    across += [(i + 1, i) for i, _ in across]

    (urgent,) = call(
        functools.partial(first_kernel, share), "first", sources, [strip],
        far_ins=range(4),
        scratch=[pltpu.VMEM((length, half), bf16)] * 2
        + [pltpu.SemaphoreType.DMA((2, ctx // 2))],
    )
    halo = lax.ppermute(urgent, "ctx", across)
    piece = shape((length, 3 * half // pieces_inside), bf16)
    query, grad, key, value, base, *sends = call(
        functools.partial(prepare_kernel, share), "prepare", (*sources, urgent),
        [block] * 4 + [strip] + [piece] * pieces_inside,
        far_ins=range(4),
        scratch=[pltpu.SemaphoreType.DMA((4, length // load_rows))],
    )
    late = lax.ppermute(base, "ctx", across)
    came = [lax.ppermute(send, "ctx", inside) for send in sends]
    cross, base_spectra = call(
        inside_kernel, "inside", (one, base, *sends, *came), [spectra, spectra]
    )

    def split(level, last):
        width, below, _ = level
        first = shape((below, taps, share), bf16 if last else f32)
        return [first] + [shape((below, taps, share), bf16)] * (width - 1)

    def partner(level, number, over=0):
        step = 2 * level[2] * number
        return [(at, at ^ step ^ over) for at in range(2 * ctx)]

    order = levels(ctx)
    keep, *sends = call(
        functools.partial(lag_kernel, order[0]), "lags",
        (one, lags, halo, cross, base_spectra),
        split(order[0], len(order) == 1),
        scratch=[pltpu.VMEM((ctx // 2, taps, share), f32)],
    )
    held = query, key, value, grad, one
    fetched = upper, lower, filter_taps
    wide = shape((2, length, channels), bf16)
    inner, upper, lower, filter_taps = call(
        functools.partial(inside_way_kernel, share), "inside_way",
        (*held, *fetched, *came, keep),
        [wide] + [shape(array.shape, bf16) for array in fetched],
        far_ins=range(5, 8),
        scratch=[pltpu.SemaphoreType.DMA((len(fetched), 4))],
        limit=large_bytes,
        flops=3 * 10**9,
    )
    held = *held, upper, lower, filter_taps
    *results, outer = call(
        functools.partial(across_first_kernel, share), "across_first",
        (*held, halo, inner, keep),
        [block] * 4 + [wide],
        far_outs=range(4),
        scratch=[pltpu.SemaphoreType.DMA((2, 4))],
        limit=large_bytes,
        flops=3 * 10**9,
    )
    for level, left in zip(order, order[1:]):
        arrived = [
            lax.ppermute(sends[number - 1], ("dp", "ctx"), partner(level, number))
            for number in (*range(2, level[0]), 1)
        ]
        below = level[1]
        keep, *sends = call(
            functools.partial(join_kernel, left, len(arrived)), "join",
            (keep, *arrived, results[0]),
            split(left, left is order[-1]),
            far_ins=(len(arrived) + 1,),
            scratch=[pltpu.VMEM((below, taps, share), f32)],
        )
    parts = [
        lax.ppermute(send, ("dp", "ctx"), partner(order[-1], number, over))
        if number or over
        else send
        for over in (0, ctx)
        for number, send in enumerate([keep] + sends)
    ]
    results = call(
        functools.partial(across_late_kernel, share), "across_late",
        (*held, late, outer, keep, *results),
        [block] * 4,
        far_ins=range(11, 15),
        far_outs=range(4),
        input_output_aliases={11 + at: at for at in range(4)},
        scratch=[
            pltpu.VMEM(wide.shape, bf16),
            pltpu.SemaphoreType.DMA((2, ctx // 2, 2)),
        ],
        limit=large_bytes,
    )
    (total,) = call(
        functools.partial(total_kernel, 1.0 / math.sqrt(2 * length * ctx)), "total",
        (*parts, results[0]),
        [shape((taps, share), f32)],
        far_ins=(len(parts),),
        far_outs=(0,),
        scratch=[pltpu.VMEM((taps, share), f32), pltpu.SemaphoreType.DMA],
    )
    return results, total


def plain(query, key, value, grad, filter_taps):
    length, channels = query.shape
    taps = filter_taps.shape[0]
    ctx = lax.axis_size("ctx")
    share = channels // ctx
    first, one, upper, lower, lags = transforms(length, taps)
    block = shape((length, channels), bf16)
    query, grad, key, value, kv, gate = call(
        plain_load_kernel, "load", (query, grad, key, value), [block] * 6,
        far_ins=range(4),
        scratch=[pltpu.SemaphoreType.DMA((4, length // load_rows))],
    )
    before, beyond = shift(kv, "ctx", 1), shift(gate, "ctx", -1)
    (sums,) = call(
        plain_lag_kernel, "lags", (one, lags, before, kv, gate), [shape((taps, channels), bf16)],
    )
    parts = jnp.transpose(sums.reshape(taps, ctx, share), (1, 0, 2))
    pieces = lax.all_to_all(parts, "ctx", 0, 0, tiled=True)
    total = sum_over_dp(jnp.sum(pieces.astype(f32), axis=0))
    total = total * (1.0 / math.sqrt(length * ctx * lax.axis_size("dp")))
    results = call(
        plain_filter_kernel, "filters",
        (first, one, upper, lower, before, kv, gate, beyond, filter_taps)
        + (query, key, value, grad),
        [block] * 4,
    )
    return results, total


def per_device(query_act, key_act, value_act, grad_out, filter_taps):
    length, channels = query_act.shape[1:]
    ctx, dp = lax.axis_size("ctx"), lax.axis_size("dp")
    share = channels // ctx
    fits = ctx & (ctx - 1) == 0 and ctx > 2 and share % lanes == 0 and tile % share == 0
    fits = fits and filter_taps.shape[0] == length and dp == 2
    run = paired if fits and channels % (2 * tile) == 0 and channels % 1024 == 0 else plain
    results, total = run(query_act[0], key_act[0], value_act[0], grad_out[0], filter_taps)
    return tuple(result[None] for result in results) + (total,)


def solution(mesh):
    sharded = P("dp", "ctx", None)
    return jax.shard_map(
        per_device,
        mesh=mesh,
        in_specs=(sharded, sharded, sharded, sharded, P()),
        out_specs=(sharded, sharded, sharded, sharded, P(None, "ctx")),
        check_vma=False,
    )
```

```python
import functools
import math

import jax
import jax.numpy as jnp
import ml_dtypes
import numpy as np
from jax import lax
from jax.experimental import pallas as pl
from jax.experimental.pallas import tpu as pltpu
from jax.sharding import PartitionSpec as P

bf16 = jnp.bfloat16
f32 = jnp.float32
small_bytes = 10 * 1024 * 1024
large_bytes = 20 * 1024 * 1024
pieces_inside = 4
tile = 512
lanes = 128
load_rows = 32
near = pl.BlockSpec(memory_space=pltpu.VMEM)
far = pl.BlockSpec(memory_space=pltpu.HBM)


def high_low(matrix):
    high = matrix.astype(ml_dtypes.bfloat16)
    low = (matrix - high.astype(np.float64)).astype(ml_dtypes.bfloat16)
    return high, low


def transforms(size, taps):
    angle = np.pi * (4 * np.arange(size) + 1) / (2 * size)
    phase = angle[:, None] * np.arange(size)[None, :]
    real, imag = np.cos(phase), np.sin(phase)
    one = np.concatenate([real, imag], axis=0)
    pair = np.concatenate([one, np.concatenate([-imag, real], axis=0)], axis=1)
    upper = np.concatenate([-imag.T, real.T], axis=1) / size
    lower = np.concatenate([real.T, imag.T], axis=1) / size
    lag = (size - np.arange(taps))[:, None] * angle[None, :]
    lags = np.concatenate([np.cos(lag), np.sin(lag)], axis=1) / size
    turned = np.concatenate([imag.T, -real.T], axis=1)[:taps] / size

    def forward(matrix):
        return np.concatenate(high_low(matrix), axis=1)

    def inverse(matrix):
        high, low = high_low(matrix)
        return np.concatenate([high, high, low], axis=1)

    return (
        forward(one[:, :taps]),
        forward(one),
        forward(pair),
        inverse(upper),
        inverse(lower),
        np.stack([inverse(lags), inverse(turned)]),
    )


def spectrum(matrix, *blocks):
    stacked = jnp.concatenate(blocks + blocks, axis=0)
    both = jnp.dot(matrix, stacked, preferred_element_type=f32)
    half = both.shape[0] // 2
    return both[:half], both[half:]


def back(matrix, real, imag):
    both = jnp.concatenate([real, imag], axis=0)
    high = both.astype(bf16)
    low = (both - high.astype(f32)).astype(bf16)
    return jnp.dot(
        matrix, jnp.concatenate([high, low, high], axis=0), preferred_element_type=f32
    )


def times(left, right):
    (lr, li), (rr, ri) = left, right
    return lr * rr - li * ri, lr * ri + li * rr


def times_conjugate(left, right):
    (lr, li), (rr, ri) = left, right
    return lr * rr + li * ri, li * rr - lr * ri


def product(left, right):
    return (left.astype(f32) * right.astype(f32)).astype(bf16)


def forward_strip(pair, upper, before, kv, weights, query, grad):
    mixed = back(upper, *times(spectrum(pair, before, kv), weights))
    return (query.astype(f32) * mixed).astype(bf16), (grad.astype(f32) * mixed).astype(bf16)


def backward_strip(pair, lower, gate, beyond, weights, key, value):
    flowing = back(lower, *times_conjugate(spectrum(pair, gate, beyond), weights))
    return (flowing * value.astype(f32)).astype(bf16), (flowing * key.astype(f32)).astype(bf16)


def tiles(ref):
    return [slice(at, at + tile) for at in range(0, ref.shape[1], tile)]


def halves(ref):
    size = ref.shape[0] // 2
    return slice(0, size), slice(size, 2 * size)


def core():
    return lax.rem(lax.axis_index("ctx"), 2)


def column_tiles(ref, body):
    def step(number, carry):
        body(number, pl.ds(pl.multiple_of(number * tile, tile), tile))
        return carry

    lax.fori_loop(0, ref.shape[-1] // tile, step, 0)


def blocks(parity, number, share):
    starts = [
        2 * number * tile + (2 * place + parity) * share for place in range(tile // share)
    ]
    if isinstance(number, int):
        return [slice(start, start + share) for start in starts]
    return [pl.ds(pl.multiple_of(start, lanes), share) for start in starts]


def gather(ref, columns):
    return jnp.concatenate([ref[:, cols] for cols in columns], axis=1)


def take(pieces, start, stop):
    width = pieces[0].shape[1]
    return jnp.concatenate(
        [
            pieces[at // width][:, at % width : at % width + lanes]
            for at in range(start, stop, lanes)
        ],
        axis=1,
    )


def wait(copies):
    for copy in copies:
        copy.wait()


def first_kernel(share, query, grad, key, value, out, left, right, sems):
    count = out.shape[1] // share

    def copies(pair, parity):
        return [
            pltpu.make_async_copy(
                source.at[:, (2 * place + parity) * share : (2 * place + parity + 1) * share],
                held.at[:, place * share : (place + 1) * share],
                sems.at[which, place],
            )
            for place in range(count)
            for which, (source, held) in enumerate(zip(pair, (left, right)))
        ]

    for parity, pair in enumerate(((query, grad), (key, value))):

        @pl.when(core() == parity)
        def _():
            for copy in copies(pair, 1 - parity):
                copy.start()

    for place, copy in enumerate(copies((key, value), 0)):
        copy.wait()
        if place % 2:
            cols = slice(place // 2 * share, (place // 2 + 1) * share)
            out[:, cols] = product(left[:, cols], right[:, cols])


def start_loads(sources, held, sems):
    rows = [slice(at, at + load_rows) for at in range(0, held[0].shape[0], load_rows)]
    groups = [
        [
            pltpu.make_async_copy(source.at[part], place.at[part], sems.at[which, number])
            for which, (source, place) in enumerate(zip(sources, held))
        ]
        for number, part in enumerate(rows)
    ]
    for group in groups:
        for copy in group:
            copy.start()
    return rows, groups


def prepare_kernel(share, *refs):
    sources, held, base, sends, sems = refs[:4], refs[5:9], refs[9], refs[10:-1], refs[-1]
    query, grad, key, value = held
    half, width = base.shape[1], sends[0].shape[1]
    rows, groups = start_loads(sources, held, sems)

    def run(parity):
        pairs = (key, value), (query, grad)
        first, second = pairs if parity == 0 else pairs[::-1]
        for part, group in zip(rows, groups):
            wait(group)
            for offset in range(0, half, lanes):
                start = 2 * (offset // share) * share + offset % share
                own = slice(start + parity * share, start + parity * share + lanes)
                other = slice(start + (1 - parity) * share, start + (1 - parity) * share + lanes)

                def put(ref, at, pair, cols):
                    ref[part, at : at + lanes] = product(pair[0][part, cols], pair[1][part, cols])

                put(base, offset, second, own)
                for number, (pair, cols) in enumerate(
                    ((second, other), (first, other), (first, own))
                ):
                    where = number * half + offset
                    put(sends[where // width], where % width, pair, cols)

    for parity in range(2):
        pl.when(core() == parity)(functools.partial(run, parity))


def inside_kernel(one, base, *refs):
    sends, came = refs[:pieces_inside], refs[pieces_inside : 2 * pieces_inside]
    cross, spectra = refs[2 * pieces_inside :]
    sign = 1.0 - 2.0 * core().astype(f32)
    real, imag = halves(cross)
    half = base.shape[1]
    for cols in tiles(base):
        low, high = cols.start, cols.stop
        own_first = spectrum(one[...], take(sends, 2 * half + low, 2 * half + high))
        own_base = spectrum(one[...], base[:, cols])
        other_first = spectrum(one[...], take(came, low, high))
        other_base = spectrum(one[...], take(came, half + low, half + high))
        spectra[real, cols], spectra[imag, cols] = own_base
        ar, ai = times_conjugate(own_first, own_base)
        both = own_first[0] - sign * other_first[1], own_first[1] + sign * other_first[0]
        br, bi = times_conjugate(both, other_base)
        cross[real, cols] = br - sign * ai
        cross[imag, cols] = bi + sign * ar


def divide(totals, sends, level):
    width, below, here = level
    own = lax.rem(lax.div(lax.axis_index("ctx"), 2 * here), width)
    for number, send in enumerate(sends):
        other = jnp.bitwise_xor(own, number)
        for place in range(below):
            send[place] = totals[other * below + place].astype(send.dtype)


def rows_of(array, count):
    size = array.shape[0] // count
    return [slice(at, at + size) for at in range(0, array.shape[0], size)]


def lag_kernel(level, one, lags, halo, cross, spectra, *refs):
    sends, totals = refs[:-1], refs[-1]
    real, imag = halves(cross)
    share = totals.shape[2]
    matrix = lags[core()]
    for cols in tiles(halo):
        ar, ai = times_conjugate(
            spectrum(one[...], halo[:, cols]), (spectra[real, cols], spectra[imag, cols])
        )
        sums = back(matrix, cross[real, cols] + ar, cross[imag, cols] + ai)
        for start in range(0, tile, share):
            totals[(cols.start + start) // share] = sums[:, start : start + share]
    divide(totals, sends, level)


def join_kernel(level, came, keep, *refs):
    arrived, sends, totals = refs[:came], refs[came + 1 : -1], refs[-1]
    for place in range(totals.shape[0]):
        value = keep[place]
        for part in arrived:
            value = value + part[place].astype(f32)
        totals[place] = value
    divide(totals, sends, level)


def total_kernel(scale, *refs):
    parts, (out, held, sem) = refs[:-4], refs[-3:]
    planes = []
    for plane in (parts[: len(parts) // 2], parts[len(parts) // 2 :]):
        value = plane[0][0].astype(f32)
        for part in plane[1:]:
            value = value + part[0].astype(f32)
        planes.append(value)
    held[...] = (planes[0] + planes[1]) * scale
    copy = pltpu.make_async_copy(held, out, sem)
    copy.start()
    copy.wait()


def spread(held, results, columns, share):
    for which, result in enumerate(results):
        for number, cols in enumerate(columns):
            held[which, :, cols] = result[:, number * share : (number + 1) * share]


def inside_way_kernel(share, query, key, value, grad, one, *refs):
    fetched, came, refs = refs[:4], refs[4 : 4 + pieces_inside], refs[5 + pieces_inside :]
    held, *placed, sems = refs
    pair, upper, lower, taps = placed
    half = taps.shape[1] // 2
    fetches = [
        pltpu.make_async_copy(source.at[rows], place.at[rows], sems.at[number, part])
        for number, (source, place) in enumerate(zip(fetched, placed))
        for part, rows in enumerate(rows_of(place, sems.shape[1]))
    ]
    for fetch in fetches:
        fetch.start()
    wait(fetches)

    def run(parity):
        for number in range(half // tile):
            for side in (parity, 1 - parity):
                columns = blocks(side, number, share)
                start = (half if side == parity else 2 * half) + number * tile
                halo = take(came, start, start + tile)
                weights = spectrum(one[...], gather(taps, columns))
                around = gather(query, columns), gather(grad, columns)
                within = gather(key, columns), gather(value, columns)
                if parity == 0:
                    results = backward_strip(
                        pair[...], lower[...], product(*around), halo, weights, *within
                    )
                else:
                    results = forward_strip(
                        pair[...], upper[...], halo, product(*within), weights, *around
                    )
                spread(held, results, columns, share)

    for parity in range(2):
        pl.when(core() == parity)(functools.partial(run, parity))


def across_way(share, late, parity, held, after, *refs):
    query, key, value, grad, one, pair, upper, lower, taps, halo = refs

    def body(number, packed):
        columns = blocks(1 - parity if late else parity, number, share)
        weights = spectrum(one[...], gather(taps, columns))
        around = gather(query, columns), gather(grad, columns)
        within = gather(key, columns), gather(value, columns)
        if parity == 0:
            results = forward_strip(
                pair[...], upper[...], halo[:, packed], product(*within), weights, *around
            )
        else:
            results = backward_strip(
                pair[...], lower[...], product(*around), halo[:, packed], weights, *within
            )
        spread(held, results, columns, share)
        after(number)

    column_tiles(halo, body)


def across_first_kernel(share, *refs):
    inputs, before, refs = refs[:10], refs[10], refs[12:]
    outs, held, sems = refs[:4], refs[4], refs[5]

    def run(parity):
        inner = outs[2:] if parity == 0 else outs[:2]
        copies = [
            pltpu.make_async_copy(before.at[which, rows], out.at[rows], sems.at[which, part])
            for which, out in enumerate(inner)
            for part, rows in enumerate(rows_of(out, sems.shape[1]))
        ]
        for copy in copies:
            copy.start()
        across_way(share, False, parity, held, lambda number: None, *inputs)
        wait(copies)

    for parity in range(2):
        pl.when(core() == parity)(functools.partial(run, parity))


def across_late_kernel(share, *refs):
    inputs, refs = refs[:10], refs[16:]
    outs, held, sems = refs[:4], refs[4], refs[5]

    def run(parity):
        outer = outs[:2] if parity == 0 else outs[2:]

        def copies(number):
            cols = pl.ds(pl.multiple_of(2 * number * tile, lanes), 2 * tile)
            return [
                pltpu.make_async_copy(
                    held.at[which, rows, cols], out.at[rows, cols], sems.at[number, which, part]
                )
                for which, out in enumerate(outer)
                for part, rows in enumerate(rows_of(out, sems.shape[2]))
            ]

        def start(number):
            for copy in copies(number):
                copy.start()

        across_way(share, True, parity, held, start, *inputs)
        for number in range(inputs[-1].shape[1] // tile):
            wait(copies(number))

    for parity in range(2):
        pl.when(core() == parity)(functools.partial(run, parity))


def plain_load_kernel(*refs):
    query, grad, key, value, kv, gate, sems = refs[4:]
    rows, groups = start_loads(refs[:4], refs[4:8], sems)
    for part, group in zip(rows, groups):
        wait(group)
        kv[part] = product(key[part], value[part])
        gate[part] = product(query[part], grad[part])


def plain_lag_kernel(one, pair, lags, before, kv, gate, sums):
    for cols in tiles(kv):
        both = spectrum(pair[...], before[:, cols], kv[:, cols])
        values = back(lags[0], *times_conjugate(both, spectrum(one[...], gate[:, cols])))
        sums[:, cols] = values.astype(bf16)


def plain_filter_kernel(
    first, pair, upper, lower, before, kv, gate, beyond, taps, query, key, value, grad,
    output, grad_query, grad_key, grad_value,
):
    for cols in tiles(kv):
        weights = spectrum(first[...], taps[:, cols])
        output[:, cols], grad_query[:, cols] = forward_strip(
            pair[...], upper[...], before[:, cols], kv[:, cols], weights,
            query[:, cols], grad[:, cols],
        )
        grad_key[:, cols], grad_value[:, cols] = backward_strip(
            pair[...], lower[...], gate[:, cols], beyond[:, cols], weights,
            key[:, cols], value[:, cols],
        )


def call(
    kernel, name, inputs, outs, scratch=(), far_ins=(), any_ins=(), far_outs=(),
    limit=small_bytes, flops=0, **more
):
    def space(at):
        return pl.ANY if at in any_ins else pltpu.HBM if at in far_ins else pltpu.VMEM

    inputs = [
        pltpu.with_memory_space_constraint(array, space(at)) for at, array in enumerate(inputs)
    ]
    return pl.pallas_call(
        kernel,
        in_specs=[pl.BlockSpec(memory_space=space(at)) for at in range(len(inputs))],
        out_specs=[far if at in far_outs else near for at in range(len(outs))],
        out_shape=[
            (pltpu.HBM if at in far_outs else pltpu.VMEM)(out.shape, out.dtype)
            for at, out in enumerate(outs)
        ],
        scratch_shapes=scratch,
        cost_estimate=pl.CostEstimate(flops=flops, bytes_accessed=0, transcendentals=0),
        compiler_params=pltpu.CompilerParams(vmem_limit_bytes=limit),
        name=name,
        **more,
    )(*inputs)


def shift(array, axis, by):
    devices = lax.axis_size(axis)
    return lax.ppermute(
        array, axis, [(i, i + by) for i in range(devices) if 0 <= i + by < devices]
    )


def sum_over_dp(own):
    dp = lax.axis_size("dp")
    if dp == 1:
        return own
    if dp == 2:
        return own + lax.ppermute(own, "dp", [(0, 1), (1, 0)])
    came = [own] + [
        lax.ppermute(own, "dp", [(i, (i + by) % dp) for i in range(dp)]) for by in range(1, dp)
    ]
    order = lax.rem(lax.axis_index("dp") - jnp.arange(dp) + dp, dp)
    return jnp.sum(jnp.stack(came)[order], axis=0)


def shape(dims, dtype):
    return jax.ShapeDtypeStruct(dims, dtype)


def levels(ctx):
    chips, found = ctx // 2, []
    while chips > 1:
        width = 4 if chips % 4 == 0 else 2
        chips //= width
        found.append((width, chips, chips))
    return found


def paired(query, key, value, grad, filter_taps):
    length, channels = query.shape
    taps = filter_taps.shape[0]
    ctx = lax.axis_size("ctx")
    share = channels // ctx
    half = channels // 2
    _, one, pair, upper, lower, lags = transforms(length, taps)
    block, strip = shape((length, channels), bf16), shape((length, half), bf16)
    spectra = shape((2 * length, half), f32)
    sources = query, grad, key, value
    inside = [(i, i ^ 1) for i in range(ctx)]
    across = [(i, i + 1) for i in range(1, ctx - 1, 2)]
    across += [(i + 1, i) for i, _ in across]

    (urgent,) = call(
        functools.partial(first_kernel, share), "first", sources, [strip],
        far_ins=range(4),
        scratch=[pltpu.VMEM((length, half), bf16)] * 2
        + [pltpu.SemaphoreType.DMA((2, ctx // 2))],
    )
    halo = lax.ppermute(urgent, "ctx", across)
    piece = shape((length, 3 * half // pieces_inside), bf16)
    query, grad, key, value, base, *sends = call(
        functools.partial(prepare_kernel, share), "prepare", (*sources, urgent),
        [block] * 4 + [strip] + [piece] * pieces_inside,
        far_ins=range(4),
        scratch=[pltpu.SemaphoreType.DMA((4, length // load_rows))],
    )
    late = lax.ppermute(base, "ctx", across)
    came = [lax.ppermute(send, "ctx", inside) for send in sends]
    cross, base_spectra = call(
        inside_kernel, "inside", (one, base, *sends, *came), [spectra, spectra]
    )

    def split(level, last):
        width, below, _ = level
        first = shape((below, taps, share), bf16 if last else f32)
        return [first] + [shape((below, taps, share), bf16)] * (width - 1)

    def partner(level, number, over=0):
        step = 2 * level[2] * number
        return [(at, at ^ step ^ over) for at in range(2 * ctx)]

    order = levels(ctx)
    keep, *sends = call(
        functools.partial(lag_kernel, order[0]), "lags",
        (one, lags, halo, cross, base_spectra),
        split(order[0], len(order) == 1),
        scratch=[pltpu.VMEM((ctx // 2, taps, share), f32)],
    )
    held = query, key, value, grad, one
    fetched = pair, upper, lower, filter_taps
    wide = shape((2, length, channels), bf16)
    inner, *fetched = call(
        functools.partial(inside_way_kernel, share), "inside_way",
        (*held, *fetched, *came, keep),
        [wide] + [shape(array.shape, bf16) for array in fetched],
        far_ins=range(5, 9),
        scratch=[pltpu.SemaphoreType.DMA((len(fetched), 4))],
        limit=large_bytes,
        flops=3 * 10**9,
    )
    held = *held, *fetched
    *results, outer = call(
        functools.partial(across_first_kernel, share), "across_first",
        (*held, halo, inner, keep),
        [block] * 4 + [wide],
        far_outs=range(4),
        scratch=[pltpu.SemaphoreType.DMA((2, 4))],
        limit=large_bytes,
        flops=3 * 10**9,
    )
    for level, left in zip(order, order[1:]):
        arrived = [
            lax.ppermute(sends[number - 1], ("dp", "ctx"), partner(level, number))
            for number in (*range(2, level[0]), 1)
        ]
        below = level[1]
        keep, *sends = call(
            functools.partial(join_kernel, left, len(arrived)), "join",
            (keep, *arrived, results[0]),
            split(left, left is order[-1]),
            far_ins=(len(arrived) + 1,),
            scratch=[pltpu.VMEM((below, taps, share), f32)],
        )
    parts = [
        lax.ppermute(send, ("dp", "ctx"), partner(order[-1], number, over))
        if number or over
        else send
        for over in (0, ctx)
        for number, send in enumerate([keep] + sends)
    ]
    *results, _ = call(
        functools.partial(across_late_kernel, share), "across_late",
        (*held, late, keep, *results, outer),
        [block] * 4 + [wide],
        far_ins=range(11, 15),
        far_outs=range(4),
        input_output_aliases={11 + at: at for at in range(5)},
        scratch=[pltpu.SemaphoreType.DMA((half // tile, 2, 2))],
        limit=large_bytes,
    )
    (total,) = call(
        functools.partial(total_kernel, 1.0 / math.sqrt(2 * length * ctx)), "total",
        (*parts, results[0]),
        [shape((taps, share), f32)],
        far_ins=(len(parts),),
        far_outs=(0,),
        scratch=[pltpu.VMEM((taps, share), f32), pltpu.SemaphoreType.DMA],
    )
    return results, total


def plain(query, key, value, grad, filter_taps):
    length, channels = query.shape
    taps = filter_taps.shape[0]
    ctx = lax.axis_size("ctx")
    share = channels // ctx
    first, one, pair, upper, lower, lags = transforms(length, taps)
    block = shape((length, channels), bf16)
    query, grad, key, value, kv, gate = call(
        plain_load_kernel, "load", (query, grad, key, value), [block] * 6,
        far_ins=range(4),
        scratch=[pltpu.SemaphoreType.DMA((4, length // load_rows))],
    )
    before, beyond = shift(kv, "ctx", 1), shift(gate, "ctx", -1)
    (sums,) = call(
        plain_lag_kernel, "lags", (one, pair, lags, before, kv, gate), [shape((taps, channels), bf16)],
    )
    parts = jnp.transpose(sums.reshape(taps, ctx, share), (1, 0, 2))
    pieces = lax.all_to_all(parts, "ctx", 0, 0, tiled=True)
    total = sum_over_dp(jnp.sum(pieces.astype(f32), axis=0))
    total = total * (1.0 / math.sqrt(length * ctx * lax.axis_size("dp")))
    results = call(
        plain_filter_kernel, "filters",
        (first, pair, upper, lower, before, kv, gate, beyond, filter_taps)
        + (query, key, value, grad),
        [block] * 4,
    )
    return results, total


def per_device(query_act, key_act, value_act, grad_out, filter_taps):
    length, channels = query_act.shape[1:]
    ctx, dp = lax.axis_size("ctx"), lax.axis_size("dp")
    share = channels // ctx
    fits = ctx & (ctx - 1) == 0 and ctx > 2 and share % lanes == 0 and tile % share == 0
    fits = fits and filter_taps.shape[0] == length and dp == 2
    run = paired if fits and channels % (2 * tile) == 0 and channels % 1024 == 0 else plain
    results, total = run(query_act[0], key_act[0], value_act[0], grad_out[0], filter_taps)
    return tuple(result[None] for result in results) + (total,)


def solution(mesh):
    sharded = P("dp", "ctx", None)
    return jax.shard_map(
        per_device,
        mesh=mesh,
        in_specs=(sharded, sharded, sharded, sharded, P()),
        out_specs=(sharded, sharded, sharded, sharded, P(None, "ctx")),
        check_vma=False,
    )
```

```python
import functools
import math

import jax
import jax.numpy as jnp
import ml_dtypes
import numpy as np
from jax import lax
from jax.experimental import pallas as pl
from jax.experimental.pallas import tpu as pltpu
from jax.sharding import PartitionSpec as P

bf16 = jnp.bfloat16
f32 = jnp.float32
small_bytes = 10 * 1024 * 1024
large_bytes = 20 * 1024 * 1024
pieces_inside = 4
tile = 512
lanes = 128
load_rows = 32
near = pl.BlockSpec(memory_space=pltpu.VMEM)
far = pl.BlockSpec(memory_space=pltpu.HBM)


def high_low(matrix):
    high = matrix.astype(ml_dtypes.bfloat16)
    low = (matrix - high.astype(np.float64)).astype(ml_dtypes.bfloat16)
    return high, low


def transforms(size, taps):
    angle = np.pi * (4 * np.arange(size) + 1) / (2 * size)
    phase = angle[:, None] * np.arange(size)[None, :]
    real, imag = np.cos(phase), np.sin(phase)
    one = np.concatenate([real, imag], axis=0)
    pair = np.concatenate([one, np.concatenate([-imag, real], axis=0)], axis=1)
    lag = (size - np.arange(taps))[:, None] * angle[None, :]
    lags = np.concatenate([np.cos(lag), np.sin(lag)], axis=1) / size
    turned = np.concatenate([imag.T, -real.T], axis=1)[:taps] / size

    def forward(matrix):
        return np.concatenate(high_low(matrix), axis=1)

    def inverse(matrix):
        high, low = high_low(matrix)
        return np.concatenate([high, high, low], axis=1)

    return (
        forward(one[:, :taps]),
        forward(one),
        forward(pair),
        np.stack([inverse(lags), inverse(turned)]),
    )


def spectrum(matrix, *blocks):
    stacked = jnp.concatenate(blocks + blocks, axis=0)
    both = jnp.dot(matrix, stacked, preferred_element_type=f32)
    half = both.shape[0] // 2
    return both[:half], both[half:]


def back(matrix, real, imag):
    both = jnp.concatenate([real, imag], axis=0)
    high = both.astype(bf16)
    low = (both - high.astype(f32)).astype(bf16)
    return jnp.dot(
        matrix, jnp.concatenate([high, low, high], axis=0), preferred_element_type=f32
    )


def times(left, right):
    (lr, li), (rr, ri) = left, right
    return lr * rr - li * ri, lr * ri + li * rr


def times_conjugate(left, right):
    (lr, li), (rr, ri) = left, right
    return lr * rr + li * ri, li * rr - lr * ri


def product(left, right):
    return (left.astype(f32) * right.astype(f32)).astype(bf16)


def forward_strip(pair, turned, before, kv, weights, query, grad):
    mixed = -back(turned, *times(spectrum(pair, before, kv), weights))
    return (query.astype(f32) * mixed).astype(bf16), (grad.astype(f32) * mixed).astype(bf16)


def backward_strip(pair, turned, gate, beyond, weights, key, value):
    real, imag = times_conjugate(spectrum(pair, gate, beyond), weights)
    flowing = back(turned, imag, -real)
    return (flowing * value.astype(f32)).astype(bf16), (flowing * key.astype(f32)).astype(bf16)


def tiles(ref):
    return [slice(at, at + tile) for at in range(0, ref.shape[1], tile)]


def halves(ref):
    size = ref.shape[0] // 2
    return slice(0, size), slice(size, 2 * size)


def core():
    return lax.rem(lax.axis_index("ctx"), 2)


def column_tiles(ref, body):
    def step(number, carry):
        body(number, pl.ds(pl.multiple_of(number * tile, tile), tile))
        return carry

    lax.fori_loop(0, ref.shape[-1] // tile, step, 0)


def blocks(parity, number, share):
    starts = [
        2 * number * tile + (2 * place + parity) * share for place in range(tile // share)
    ]
    if isinstance(number, int):
        return [slice(start, start + share) for start in starts]
    return [pl.ds(pl.multiple_of(start, lanes), share) for start in starts]


def gather(ref, columns):
    return jnp.concatenate([ref[:, cols] for cols in columns], axis=1)


def take(pieces, start, stop):
    width = pieces[0].shape[1]
    return jnp.concatenate(
        [
            pieces[at // width][:, at % width : at % width + lanes]
            for at in range(start, stop, lanes)
        ],
        axis=1,
    )


def wait(copies):
    for copy in copies:
        copy.wait()


def first_kernel(share, query, grad, key, value, out, left, right, sems):
    count = out.shape[1] // share

    def copies(pair, parity):
        return [
            pltpu.make_async_copy(
                source.at[:, (2 * place + parity) * share : (2 * place + parity + 1) * share],
                held.at[:, place * share : (place + 1) * share],
                sems.at[which, place],
            )
            for place in range(count)
            for which, (source, held) in enumerate(zip(pair, (left, right)))
        ]

    for parity, pair in enumerate(((query, grad), (key, value))):

        @pl.when(core() == parity)
        def _():
            for copy in copies(pair, 1 - parity):
                copy.start()

    for place, copy in enumerate(copies((key, value), 0)):
        copy.wait()
        if place % 2:
            cols = slice(place // 2 * share, (place // 2 + 1) * share)
            out[:, cols] = product(left[:, cols], right[:, cols])


def start_loads(sources, held, sems):
    rows = [slice(at, at + load_rows) for at in range(0, held[0].shape[0], load_rows)]
    groups = [
        [
            pltpu.make_async_copy(source.at[part], place.at[part], sems.at[which, number])
            for which, (source, place) in enumerate(zip(sources, held))
        ]
        for number, part in enumerate(rows)
    ]
    for group in groups:
        for copy in group:
            copy.start()
    return rows, groups


def prepare_kernel(share, *refs):
    sources, held, base, sends = refs[:4], refs[5:9], refs[9], refs[10:]
    query, grad, key, value = sources
    half, width = base.shape[1], sends[0].shape[1]

    def run(parity):
        pairs = (key, value), (query, grad)
        first, second = pairs if parity == 0 else pairs[::-1]
        for part in rows_of(base, base.shape[0] // load_rows):
            for source, place in zip(sources, held):
                place[part] = source[part]
            for offset in range(0, half, lanes):
                start = 2 * (offset // share) * share + offset % share
                own = slice(start + parity * share, start + parity * share + lanes)
                other = slice(start + (1 - parity) * share, start + (1 - parity) * share + lanes)

                def put(ref, at, pair, cols):
                    ref[part, at : at + lanes] = product(pair[0][part, cols], pair[1][part, cols])

                put(base, offset, second, own)
                for number, (pair, cols) in enumerate(
                    ((second, other), (first, other), (first, own))
                ):
                    where = number * half + offset
                    put(sends[where // width], where % width, pair, cols)

    for parity in range(2):
        pl.when(core() == parity)(functools.partial(run, parity))


def inside_kernel(one, base, *refs):
    sends, came = refs[:pieces_inside], refs[pieces_inside : 2 * pieces_inside]
    cross, spectra = refs[2 * pieces_inside :]
    sign = 1.0 - 2.0 * core().astype(f32)
    real, imag = halves(cross)
    half = base.shape[1]
    for cols in tiles(base):
        low, high = cols.start, cols.stop
        own_first = spectrum(one[...], take(sends, 2 * half + low, 2 * half + high))
        own_base = spectrum(one[...], base[:, cols])
        other_first = spectrum(one[...], take(came, low, high))
        other_base = spectrum(one[...], take(came, half + low, half + high))
        spectra[real, cols], spectra[imag, cols] = own_base
        ar, ai = times_conjugate(own_first, own_base)
        both = own_first[0] - sign * other_first[1], own_first[1] + sign * other_first[0]
        br, bi = times_conjugate(both, other_base)
        cross[real, cols] = br - sign * ai
        cross[imag, cols] = bi + sign * ar


def divide(totals, sends, level):
    width, below, here = level
    own = lax.rem(lax.div(lax.axis_index("ctx"), 2 * here), width)
    for number, send in enumerate(sends):
        other = jnp.bitwise_xor(own, number)
        for place in range(below):
            send[place] = totals[other * below + place].astype(send.dtype)


def rows_of(array, count):
    size = array.shape[0] // count
    return [slice(at, at + size) for at in range(0, array.shape[0], size)]


def lag_kernel(level, one, lags, halo, cross, spectra, *refs):
    sends, totals = refs[:-1], refs[-1]
    real, imag = halves(cross)
    share = totals.shape[2]
    matrix = lags[core()]
    for cols in tiles(halo):
        ar, ai = times_conjugate(
            spectrum(one[...], halo[:, cols]), (spectra[real, cols], spectra[imag, cols])
        )
        sums = back(matrix, cross[real, cols] + ar, cross[imag, cols] + ai)
        for start in range(0, tile, share):
            totals[(cols.start + start) // share] = sums[:, start : start + share]
    divide(totals, sends, level)


def join_kernel(level, came, keep, *refs):
    arrived, sends, totals = refs[:came], refs[came + 1 : -1], refs[-1]
    for place in range(totals.shape[0]):
        value = keep[place]
        for part in arrived:
            value = value + part[place].astype(f32)
        totals[place] = value
    divide(totals, sends, level)


def total_kernel(scale, *refs):
    parts, (out, held, sem) = refs[:-4], refs[-3:]
    planes = []
    for plane in (parts[: len(parts) // 2], parts[len(parts) // 2 :]):
        value = plane[0][0].astype(f32)
        for part in plane[1:]:
            value = value + part[0].astype(f32)
        planes.append(value)
    held[...] = (planes[0] + planes[1]) * scale
    copy = pltpu.make_async_copy(held, out, sem)
    copy.start()
    copy.wait()


def spread(held, results, columns, share):
    for which, result in enumerate(results):
        for number, cols in enumerate(columns):
            held[which, :, cols] = result[:, number * share : (number + 1) * share]


def make_pair(one, pair):
    size = one.shape[0] // 2
    for part in range(2):
        real = one[:size, part * size : (part + 1) * size]
        imag = one[size:, part * size : (part + 1) * size]
        start = 2 * part * size
        pair[:size, start : start + size] = real
        pair[size:, start : start + size] = imag
        pair[:size, start + size : start + 2 * size] = -imag
        pair[size:, start + size : start + 2 * size] = real


def inside_way_kernel(share, query, key, value, grad, one, lags, taps_in, *refs):
    came, (held, pair, taps) = refs[:pieces_inside], refs[1 + pieces_inside :]
    half = taps.shape[1] // 2
    taps[...] = taps_in[...]
    make_pair(one, pair)

    def run(parity):
        for number in range(half // tile):
            for side in (parity, 1 - parity):
                columns = blocks(side, number, share)
                start = (half if side == parity else 2 * half) + number * tile
                halo = take(came, start, start + tile)
                weights = spectrum(one[...], gather(taps, columns))
                around = gather(query, columns), gather(grad, columns)
                within = gather(key, columns), gather(value, columns)
                if parity == 0:
                    results = backward_strip(
                        pair[...], lags[1], product(*around), halo, weights, *within
                    )
                else:
                    results = forward_strip(
                        pair[...], lags[1], halo, product(*within), weights, *around
                    )
                spread(held, results, columns, share)

    for parity in range(2):
        pl.when(core() == parity)(functools.partial(run, parity))


def across_way(share, late, parity, held, after, *refs):
    query, key, value, grad, one, lags, pair, taps, halo = refs

    def body(number, packed):
        columns = blocks(1 - parity if late else parity, number, share)
        weights = spectrum(one[...], gather(taps, columns))
        around = gather(query, columns), gather(grad, columns)
        within = gather(key, columns), gather(value, columns)
        if parity == 0:
            results = forward_strip(
                pair[...], lags[1], halo[:, packed], product(*within), weights, *around
            )
        else:
            results = backward_strip(
                pair[...], lags[1], product(*around), halo[:, packed], weights, *within
            )
        spread(held, results, columns, share)
        after(number)

    column_tiles(halo, body)


def across_first_kernel(share, *refs):
    inputs, before, refs = refs[:9], refs[9], refs[11:]
    outs, held, sems = refs[:4], refs[4], refs[5]

    def run(parity):
        inner = outs[2:] if parity == 0 else outs[:2]
        copies = [
            pltpu.make_async_copy(before.at[which, rows], out.at[rows], sems.at[which, part])
            for which, out in enumerate(inner)
            for part, rows in enumerate(rows_of(out, sems.shape[1]))
        ]
        for copy in copies:
            copy.start()
        across_way(share, False, parity, held, lambda number: None, *inputs)
        wait(copies)

    for parity in range(2):
        pl.when(core() == parity)(functools.partial(run, parity))


def across_late_kernel(share, *refs):
    inputs, refs = refs[:9], refs[15:]
    outs, held, sems = refs[:4], refs[4], refs[5]

    def run(parity):
        outer = outs[:2] if parity == 0 else outs[2:]

        def copies(number):
            cols = pl.ds(pl.multiple_of(2 * number * tile, lanes), 2 * tile)
            return [
                pltpu.make_async_copy(
                    held.at[which, rows, cols], out.at[rows, cols], sems.at[number, which, part]
                )
                for which, out in enumerate(outer)
                for part, rows in enumerate(rows_of(out, sems.shape[2]))
            ]

        def start(number):
            for copy in copies(number):
                copy.start()

        across_way(share, True, parity, held, start, *inputs)
        for number in range(inputs[-1].shape[1] // tile):
            wait(copies(number))

    for parity in range(2):
        pl.when(core() == parity)(functools.partial(run, parity))


def plain_load_kernel(*refs):
    query, grad, key, value, kv, gate, sems = refs[4:]
    rows, groups = start_loads(refs[:4], refs[4:8], sems)
    for part, group in zip(rows, groups):
        wait(group)
        kv[part] = product(key[part], value[part])
        gate[part] = product(query[part], grad[part])


def plain_lag_kernel(one, pair, lags, before, kv, gate, sums):
    for cols in tiles(kv):
        both = spectrum(pair[...], before[:, cols], kv[:, cols])
        values = back(lags[0], *times_conjugate(both, spectrum(one[...], gate[:, cols])))
        sums[:, cols] = values.astype(bf16)


def plain_filter_kernel(
    first, pair, lags, before, kv, gate, beyond, taps, query, key, value, grad,
    output, grad_query, grad_key, grad_value,
):
    for cols in tiles(kv):
        weights = spectrum(first[...], taps[:, cols])
        output[:, cols], grad_query[:, cols] = forward_strip(
            pair[...], lags[1], before[:, cols], kv[:, cols], weights,
            query[:, cols], grad[:, cols],
        )
        grad_key[:, cols], grad_value[:, cols] = backward_strip(
            pair[...], lags[1], gate[:, cols], beyond[:, cols], weights,
            key[:, cols], value[:, cols],
        )


def call(
    kernel, name, inputs, outs, scratch=(), far_ins=(), any_ins=(), far_outs=(),
    limit=small_bytes, flops=0, **more
):
    def space(at):
        return pl.ANY if at in any_ins else pltpu.HBM if at in far_ins else pltpu.VMEM

    inputs = [
        pltpu.with_memory_space_constraint(array, space(at)) for at, array in enumerate(inputs)
    ]
    return pl.pallas_call(
        kernel,
        in_specs=[pl.BlockSpec(memory_space=space(at)) for at in range(len(inputs))],
        out_specs=[far if at in far_outs else near for at in range(len(outs))],
        out_shape=[
            (pltpu.HBM if at in far_outs else pltpu.VMEM)(out.shape, out.dtype)
            for at, out in enumerate(outs)
        ],
        scratch_shapes=scratch,
        cost_estimate=pl.CostEstimate(flops=flops, bytes_accessed=0, transcendentals=0),
        compiler_params=pltpu.CompilerParams(vmem_limit_bytes=limit),
        name=name,
        **more,
    )(*inputs)


def shift(array, axis, by):
    devices = lax.axis_size(axis)
    return lax.ppermute(
        array, axis, [(i, i + by) for i in range(devices) if 0 <= i + by < devices]
    )


def sum_over_dp(own):
    dp = lax.axis_size("dp")
    if dp == 1:
        return own
    if dp == 2:
        return own + lax.ppermute(own, "dp", [(0, 1), (1, 0)])
    came = [own] + [
        lax.ppermute(own, "dp", [(i, (i + by) % dp) for i in range(dp)]) for by in range(1, dp)
    ]
    order = lax.rem(lax.axis_index("dp") - jnp.arange(dp) + dp, dp)
    return jnp.sum(jnp.stack(came)[order], axis=0)


def shape(dims, dtype):
    return jax.ShapeDtypeStruct(dims, dtype)


def levels(ctx):
    chips, found = ctx // 2, []
    while chips > 1:
        width = 4 if chips % 4 == 0 else 2
        chips //= width
        found.append((width, chips, chips))
    return found


def paired(query, key, value, grad, filter_taps):
    length, channels = query.shape
    taps = filter_taps.shape[0]
    ctx = lax.axis_size("ctx")
    share = channels // ctx
    half = channels // 2
    _, one, _, lags = transforms(length, taps)
    block, strip = shape((length, channels), bf16), shape((length, half), bf16)
    spectra = shape((2 * length, half), f32)
    sources = query, grad, key, value
    inside = [(i, i ^ 1) for i in range(ctx)]
    across = [(i, i + 1) for i in range(1, ctx - 1, 2)]
    across += [(i + 1, i) for i, _ in across]

    (urgent,) = call(
        functools.partial(first_kernel, share), "first", sources, [strip],
        far_ins=range(4),
        scratch=[pltpu.VMEM((length, half), bf16)] * 2
        + [pltpu.SemaphoreType.DMA((2, ctx // 2))],
    )
    halo = lax.ppermute(urgent, "ctx", across)
    piece = shape((length, 3 * half // pieces_inside), bf16)
    query, grad, key, value, base, *sends = call(
        functools.partial(prepare_kernel, share), "prepare", (*sources, urgent),
        [block] * 4 + [strip] + [piece] * pieces_inside,
    )
    late = lax.ppermute(base, "ctx", across)
    came = [lax.ppermute(send, "ctx", inside) for send in sends]
    cross, base_spectra = call(
        inside_kernel, "inside", (one, base, *sends, *came), [spectra, spectra]
    )

    def split(level, last):
        width, below, _ = level
        first = shape((below, taps, share), bf16 if last else f32)
        return [first] + [shape((below, taps, share), bf16)] * (width - 1)

    def partner(level, number, over=0):
        step = 2 * level[2] * number
        return [(at, at ^ step ^ over) for at in range(2 * ctx)]

    order = levels(ctx)
    keep, *sends = call(
        functools.partial(lag_kernel, order[0]), "lags",
        (one, lags, halo, cross, base_spectra),
        split(order[0], len(order) == 1),
        scratch=[pltpu.VMEM((ctx // 2, taps, share), f32)],
    )
    held = query, key, value, grad, one, lags
    wide = shape((2, length, channels), bf16)
    inner, *made = call(
        functools.partial(inside_way_kernel, share), "inside_way",
        (*held, filter_taps, *came, keep),
        [wide, shape((2 * length, 4 * length), bf16), block],
        limit=large_bytes,
        flops=3 * 10**9,
    )
    held = *held, *made
    *results, outer = call(
        functools.partial(across_first_kernel, share), "across_first",
        (*held, halo, inner, keep),
        [block] * 4 + [wide],
        far_outs=range(4),
        scratch=[pltpu.SemaphoreType.DMA((2, 4))],
        limit=large_bytes,
        flops=3 * 10**9,
    )
    for level, left in zip(order, order[1:]):
        arrived = [
            lax.ppermute(sends[number - 1], ("dp", "ctx"), partner(level, number))
            for number in (*range(2, level[0]), 1)
        ]
        below = level[1]
        keep, *sends = call(
            functools.partial(join_kernel, left, len(arrived)), "join",
            (keep, *arrived, results[0]),
            split(left, left is order[-1]),
            far_ins=(len(arrived) + 1,),
            scratch=[pltpu.VMEM((below, taps, share), f32)],
        )
    parts = [
        lax.ppermute(send, ("dp", "ctx"), partner(order[-1], number, over))
        if number or over
        else send
        for over in (0, ctx)
        for number, send in enumerate([keep] + sends)
    ]
    *results, _ = call(
        functools.partial(across_late_kernel, share), "across_late",
        (*held, late, keep, *results, outer),
        [block] * 4 + [wide],
        far_ins=range(10, 14),
        far_outs=range(4),
        input_output_aliases={10 + at: at for at in range(5)},
        scratch=[pltpu.SemaphoreType.DMA((half // tile, 2, 2))],
        limit=large_bytes,
    )
    (total,) = call(
        functools.partial(total_kernel, 1.0 / math.sqrt(2 * length * ctx)), "total",
        (*parts, results[0]),
        [shape((taps, share), f32)],
        far_ins=(len(parts),),
        far_outs=(0,),
        scratch=[pltpu.VMEM((taps, share), f32), pltpu.SemaphoreType.DMA],
    )
    return results, total


def plain(query, key, value, grad, filter_taps):
    length, channels = query.shape
    taps = filter_taps.shape[0]
    ctx = lax.axis_size("ctx")
    share = channels // ctx
    first, one, pair, lags = transforms(length, taps)
    block = shape((length, channels), bf16)
    query, grad, key, value, kv, gate = call(
        plain_load_kernel, "load", (query, grad, key, value), [block] * 6,
        far_ins=range(4),
        scratch=[pltpu.SemaphoreType.DMA((4, length // load_rows))],
    )
    before, beyond = shift(kv, "ctx", 1), shift(gate, "ctx", -1)
    (sums,) = call(
        plain_lag_kernel, "lags", (one, pair, lags, before, kv, gate), [shape((taps, channels), bf16)],
    )
    parts = jnp.transpose(sums.reshape(taps, ctx, share), (1, 0, 2))
    pieces = lax.all_to_all(parts, "ctx", 0, 0, tiled=True)
    total = sum_over_dp(jnp.sum(pieces.astype(f32), axis=0))
    total = total * (1.0 / math.sqrt(length * ctx * lax.axis_size("dp")))
    results = call(
        plain_filter_kernel, "filters",
        (first, pair, lags, before, kv, gate, beyond, filter_taps)
        + (query, key, value, grad),
        [block] * 4,
    )
    return results, total


def per_device(query_act, key_act, value_act, grad_out, filter_taps):
    length, channels = query_act.shape[1:]
    ctx, dp = lax.axis_size("ctx"), lax.axis_size("dp")
    share = channels // ctx
    fits = ctx & (ctx - 1) == 0 and ctx > 2 and share % lanes == 0 and tile % share == 0
    fits = fits and filter_taps.shape[0] == length and dp == 2
    run = paired if fits and channels % (2 * tile) == 0 and channels % 1024 == 0 else plain
    results, total = run(query_act[0], key_act[0], value_act[0], grad_out[0], filter_taps)
    return tuple(result[None] for result in results) + (total,)


def solution(mesh):
    sharded = P("dp", "ctx", None)
    return jax.shard_map(
        per_device,
        mesh=mesh,
        in_specs=(sharded, sharded, sharded, sharded, P()),
        out_specs=(sharded, sharded, sharded, sharded, P(None, "ctx")),
        check_vma=False,
    )
```

```python
import functools
import math

import jax
import jax.numpy as jnp
import ml_dtypes
import numpy as np
from jax import lax
from jax.experimental import pallas as pl
from jax.experimental.pallas import tpu as pltpu
from jax.sharding import PartitionSpec as P

bf16 = jnp.bfloat16
f32 = jnp.float32
small_bytes = 10 * 1024 * 1024
large_bytes = 20 * 1024 * 1024
pieces_inside = 4
tile = 512
lanes = 128
load_rows = 32
near = pl.BlockSpec(memory_space=pltpu.VMEM)
far = pl.BlockSpec(memory_space=pltpu.HBM)


def high_low(matrix):
    high = matrix.astype(ml_dtypes.bfloat16)
    low = (matrix - high.astype(np.float64)).astype(ml_dtypes.bfloat16)
    return high, low


def transforms(size, taps):
    angle = np.pi * (4 * np.arange(size) + 1) / (2 * size)
    phase = angle[:, None] * np.arange(size)[None, :]
    real, imag = np.cos(phase), np.sin(phase)
    one = np.concatenate([real, imag], axis=0)
    pair = np.concatenate([one, np.concatenate([-imag, real], axis=0)], axis=1)
    lag = (size - np.arange(taps))[:, None] * angle[None, :]
    lags = np.concatenate([np.cos(lag), np.sin(lag)], axis=1) / size
    turned = np.concatenate([imag.T, -real.T], axis=1)[:taps] / size

    def forward(matrix):
        return np.concatenate(high_low(matrix), axis=1)

    def inverse(matrix):
        high, low = high_low(matrix)
        return np.concatenate([high, high, low], axis=1)

    return (
        forward(one[:, :taps]),
        forward(one),
        forward(pair),
        np.stack([inverse(lags), inverse(turned)]),
    )


def spectrum(matrix, *blocks):
    stacked = jnp.concatenate(blocks + blocks, axis=0)
    both = jnp.dot(matrix, stacked, preferred_element_type=f32)
    half = both.shape[0] // 2
    return both[:half], both[half:]


def back(matrix, real, imag):
    both = jnp.concatenate([real, imag], axis=0)
    high = both.astype(bf16)
    low = (both - high.astype(f32)).astype(bf16)
    return jnp.dot(
        matrix, jnp.concatenate([high, low, high], axis=0), preferred_element_type=f32
    )


def times(left, right):
    (lr, li), (rr, ri) = left, right
    return lr * rr - li * ri, lr * ri + li * rr


def times_conjugate(left, right):
    (lr, li), (rr, ri) = left, right
    return lr * rr + li * ri, li * rr - lr * ri


def product(left, right):
    return (left.astype(f32) * right.astype(f32)).astype(bf16)


def forward_strip(pair, turned, before, kv, weights, query, grad):
    mixed = -back(turned, *times(spectrum(pair, before, kv), weights))
    return (query.astype(f32) * mixed).astype(bf16), (grad.astype(f32) * mixed).astype(bf16)


def backward_strip(pair, turned, gate, beyond, weights, key, value):
    real, imag = times_conjugate(spectrum(pair, gate, beyond), weights)
    flowing = back(turned, imag, -real)
    return (flowing * value.astype(f32)).astype(bf16), (flowing * key.astype(f32)).astype(bf16)


def tiles(ref):
    return [slice(at, at + tile) for at in range(0, ref.shape[1], tile)]


def halves(ref):
    size = ref.shape[0] // 2
    return slice(0, size), slice(size, 2 * size)


def core():
    return lax.rem(lax.axis_index("ctx"), 2)


def column_tiles(ref, body):
    def step(number, carry):
        body(number, pl.ds(pl.multiple_of(number * tile, tile), tile))
        return carry

    lax.fori_loop(0, ref.shape[-1] // tile, step, 0)


def blocks(parity, number, share):
    starts = [
        2 * number * tile + (2 * place + parity) * share for place in range(tile // share)
    ]
    if isinstance(number, int):
        return [slice(start, start + share) for start in starts]
    return [pl.ds(pl.multiple_of(start, lanes), share) for start in starts]


def gather(ref, columns):
    return jnp.concatenate([ref[:, cols] for cols in columns], axis=1)


def take(pieces, start, stop):
    width = pieces[0].shape[1]
    return jnp.concatenate(
        [
            pieces[at // width][:, at % width : at % width + lanes]
            for at in range(start, stop, lanes)
        ],
        axis=1,
    )


def wait(copies):
    for copy in copies:
        copy.wait()


def first_kernel(share, query, grad, key, value, out, left, right, sems):
    count = out.shape[1] // share

    def copies(pair, parity):
        return [
            pltpu.make_async_copy(
                source.at[:, (2 * place + parity) * share : (2 * place + parity + 1) * share],
                held.at[:, place * share : (place + 1) * share],
                sems.at[which, place],
            )
            for place in range(count)
            for which, (source, held) in enumerate(zip(pair, (left, right)))
        ]

    for parity, pair in enumerate(((query, grad), (key, value))):

        @pl.when(core() == parity)
        def _():
            for copy in copies(pair, 1 - parity):
                copy.start()

    for place, copy in enumerate(copies((key, value), 0)):
        copy.wait()
        if place % 2:
            cols = slice(place // 2 * share, (place // 2 + 1) * share)
            out[:, cols] = product(left[:, cols], right[:, cols])


def start_loads(sources, held, sems):
    rows = [slice(at, at + load_rows) for at in range(0, held[0].shape[0], load_rows)]
    groups = [
        [
            pltpu.make_async_copy(source.at[part], place.at[part], sems.at[which, number])
            for which, (source, place) in enumerate(zip(sources, held))
        ]
        for number, part in enumerate(rows)
    ]
    for group in groups:
        for copy in group:
            copy.start()
    return rows, groups


def prepare_kernel(share, *refs):
    sources, held, base, sends = refs[:4], refs[5:9], refs[9], refs[10:]
    query, grad, key, value = sources
    half, width = base.shape[1], sends[0].shape[1]

    def run(parity):
        pairs = (key, value), (query, grad)
        first, second = pairs if parity == 0 else pairs[::-1]
        for part in rows_of(base, base.shape[0] // load_rows):
            for source, place in zip(sources, held):
                place[part] = source[part]
            for offset in range(0, half, lanes):
                start = 2 * (offset // share) * share + offset % share
                own = slice(start + parity * share, start + parity * share + lanes)
                other = slice(start + (1 - parity) * share, start + (1 - parity) * share + lanes)

                def put(ref, at, pair, cols):
                    ref[part, at : at + lanes] = product(pair[0][part, cols], pair[1][part, cols])

                put(base, offset, second, own)
                for number, (pair, cols) in enumerate(
                    ((second, other), (first, other), (first, own))
                ):
                    where = number * half + offset
                    put(sends[where // width], where % width, pair, cols)

    for parity in range(2):
        pl.when(core() == parity)(functools.partial(run, parity))


def inside_kernel(one, base, *refs):
    sends, came = refs[:pieces_inside], refs[pieces_inside : 2 * pieces_inside]
    cross, spectra = refs[2 * pieces_inside :]
    sign = 1.0 - 2.0 * core().astype(f32)
    real, imag = halves(cross)
    half = base.shape[1]
    for cols in tiles(base):
        low, high = cols.start, cols.stop
        own_first = spectrum(one[...], take(sends, 2 * half + low, 2 * half + high))
        own_base = spectrum(one[...], base[:, cols])
        other_first = spectrum(one[...], take(came, low, high))
        other_base = spectrum(one[...], take(came, half + low, half + high))
        spectra[real, cols], spectra[imag, cols] = own_base
        ar, ai = times_conjugate(own_first, own_base)
        both = own_first[0] - sign * other_first[1], own_first[1] + sign * other_first[0]
        br, bi = times_conjugate(both, other_base)
        cross[real, cols] = br - sign * ai
        cross[imag, cols] = bi + sign * ar


def divide(totals, sends, level):
    width, below, here = level
    own = lax.rem(lax.div(lax.axis_index("ctx"), 2 * here), width)
    for number, send in enumerate(sends):
        other = jnp.bitwise_xor(own, number)
        for place in range(below):
            send[place] = totals[other * below + place].astype(send.dtype)


def rows_of(array, count):
    size = array.shape[0] // count
    return [slice(at, at + size) for at in range(0, array.shape[0], size)]


def lag_kernel(level, one, lags, halo, cross, spectra, *refs):
    sends, totals = refs[:-1], refs[-1]
    real, imag = halves(cross)
    share = totals.shape[2]
    matrix = lags[core()]
    for cols in tiles(halo):
        ar, ai = times_conjugate(
            spectrum(one[...], halo[:, cols]), (spectra[real, cols], spectra[imag, cols])
        )
        sums = back(matrix, cross[real, cols] + ar, cross[imag, cols] + ai)
        for start in range(0, tile, share):
            totals[(cols.start + start) // share] = sums[:, start : start + share]
    divide(totals, sends, level)


def join_kernel(level, came, keep, *refs):
    arrived, sends, totals = refs[:came], refs[came + 1 : -1], refs[-1]
    for place in range(totals.shape[0]):
        value = keep[place]
        for part in arrived:
            value = value + part[place].astype(f32)
        totals[place] = value
    divide(totals, sends[:-1], level)
    sends[-1][...] = sends[0][...]


def total_kernel(scale, *refs):
    parts, (out, held, sem) = refs[:-4], refs[-3:]
    planes = []
    for plane in (parts[: len(parts) // 2], parts[len(parts) // 2 :]):
        value = plane[0][0].astype(f32)
        for part in plane[1:]:
            value = value + part[0].astype(f32)
        planes.append(value)
    held[...] = (planes[0] + planes[1]) * scale
    copy = pltpu.make_async_copy(held, out, sem)
    copy.start()
    copy.wait()


def spread(held, results, columns, share):
    for which, result in enumerate(results):
        for number, cols in enumerate(columns):
            held[which, :, cols] = result[:, number * share : (number + 1) * share]


def make_pair(one, pair):
    size = one.shape[0] // 2
    for part in range(2):
        real = one[:size, part * size : (part + 1) * size]
        imag = one[size:, part * size : (part + 1) * size]
        start = 2 * part * size
        pair[:size, start : start + size] = real
        pair[size:, start : start + size] = imag
        pair[:size, start + size : start + 2 * size] = -imag
        pair[size:, start + size : start + 2 * size] = real


def inside_way_kernel(share, query, key, value, grad, one, lags, taps_in, *refs):
    came, (held, pair, taps) = refs[:pieces_inside], refs[1 + pieces_inside :]
    half = taps.shape[1] // 2
    taps[...] = taps_in[...]
    make_pair(one, pair)

    def run(parity):
        for number in range(half // tile):
            for side in (parity, 1 - parity):
                columns = blocks(side, number, share)
                start = (half if side == parity else 2 * half) + number * tile
                halo = take(came, start, start + tile)
                weights = spectrum(one[...], gather(taps, columns))
                around = gather(query, columns), gather(grad, columns)
                within = gather(key, columns), gather(value, columns)
                if parity == 0:
                    results = backward_strip(
                        pair[...], lags[1], product(*around), halo, weights, *within
                    )
                else:
                    results = forward_strip(
                        pair[...], lags[1], halo, product(*within), weights, *around
                    )
                spread(held, results, columns, share)

    for parity in range(2):
        pl.when(core() == parity)(functools.partial(run, parity))


def across_way(share, late, parity, held, after, *refs):
    query, key, value, grad, one, lags, pair, taps, halo = refs

    def body(number, packed):
        columns = blocks(1 - parity if late else parity, number, share)
        weights = spectrum(one[...], gather(taps, columns))
        around = gather(query, columns), gather(grad, columns)
        within = gather(key, columns), gather(value, columns)
        if parity == 0:
            results = forward_strip(
                pair[...], lags[1], halo[:, packed], product(*within), weights, *around
            )
        else:
            results = backward_strip(
                pair[...], lags[1], product(*around), halo[:, packed], weights, *within
            )
        spread(held, results, columns, share)
        after(number)

    column_tiles(halo, body)


def across_first_kernel(share, *refs):
    inputs, before, refs = refs[:9], refs[9], refs[11:]
    outs, held, sems = refs[:4], refs[4], refs[5]

    def run(parity):
        inner = outs[2:] if parity == 0 else outs[:2]
        copies = [
            pltpu.make_async_copy(before.at[which, rows], out.at[rows], sems.at[which, part])
            for which, out in enumerate(inner)
            for part, rows in enumerate(rows_of(out, sems.shape[1]))
        ]
        for copy in copies:
            copy.start()
        across_way(share, False, parity, held, lambda number: None, *inputs)
        wait(copies)

    for parity in range(2):
        pl.when(core() == parity)(functools.partial(run, parity))


def across_late_kernel(share, *refs):
    inputs, refs = refs[:9], refs[15:]
    outs, held, sems = refs[:4], refs[4], refs[5]

    def run(parity):
        outer = outs[:2] if parity == 0 else outs[2:]

        def copies(number):
            cols = pl.ds(pl.multiple_of(2 * number * tile, lanes), 2 * tile)
            return [
                pltpu.make_async_copy(
                    held.at[which, rows, cols], out.at[rows, cols], sems.at[number, which, part]
                )
                for which, out in enumerate(outer)
                for part, rows in enumerate(rows_of(out, sems.shape[2]))
            ]

        def start(number):
            for copy in copies(number):
                copy.start()

        across_way(share, True, parity, held, start, *inputs)
        for number in range(inputs[-1].shape[1] // tile):
            wait(copies(number))

    for parity in range(2):
        pl.when(core() == parity)(functools.partial(run, parity))


def plain_load_kernel(*refs):
    query, grad, key, value, kv, gate, sems = refs[4:]
    rows, groups = start_loads(refs[:4], refs[4:8], sems)
    for part, group in zip(rows, groups):
        wait(group)
        kv[part] = product(key[part], value[part])
        gate[part] = product(query[part], grad[part])


def plain_lag_kernel(one, pair, lags, before, kv, gate, sums):
    for cols in tiles(kv):
        both = spectrum(pair[...], before[:, cols], kv[:, cols])
        values = back(lags[0], *times_conjugate(both, spectrum(one[...], gate[:, cols])))
        sums[:, cols] = values.astype(bf16)


def plain_filter_kernel(
    first, pair, lags, before, kv, gate, beyond, taps, query, key, value, grad,
    output, grad_query, grad_key, grad_value,
):
    for cols in tiles(kv):
        weights = spectrum(first[...], taps[:, cols])
        output[:, cols], grad_query[:, cols] = forward_strip(
            pair[...], lags[1], before[:, cols], kv[:, cols], weights,
            query[:, cols], grad[:, cols],
        )
        grad_key[:, cols], grad_value[:, cols] = backward_strip(
            pair[...], lags[1], gate[:, cols], beyond[:, cols], weights,
            key[:, cols], value[:, cols],
        )


def call(
    kernel, name, inputs, outs, scratch=(), far_ins=(), any_ins=(), far_outs=(),
    limit=small_bytes, flops=0, **more
):
    def space(at):
        return pl.ANY if at in any_ins else pltpu.HBM if at in far_ins else pltpu.VMEM

    inputs = [
        pltpu.with_memory_space_constraint(array, space(at)) for at, array in enumerate(inputs)
    ]
    return pl.pallas_call(
        kernel,
        in_specs=[pl.BlockSpec(memory_space=space(at)) for at in range(len(inputs))],
        out_specs=[far if at in far_outs else near for at in range(len(outs))],
        out_shape=[
            (pltpu.HBM if at in far_outs else pltpu.VMEM)(out.shape, out.dtype)
            for at, out in enumerate(outs)
        ],
        scratch_shapes=scratch,
        cost_estimate=pl.CostEstimate(flops=flops, bytes_accessed=0, transcendentals=0),
        compiler_params=pltpu.CompilerParams(vmem_limit_bytes=limit),
        name=name,
        **more,
    )(*inputs)


def shift(array, axis, by):
    devices = lax.axis_size(axis)
    return lax.ppermute(
        array, axis, [(i, i + by) for i in range(devices) if 0 <= i + by < devices]
    )


def sum_over_dp(own):
    dp = lax.axis_size("dp")
    if dp == 1:
        return own
    if dp == 2:
        return own + lax.ppermute(own, "dp", [(0, 1), (1, 0)])
    came = [own] + [
        lax.ppermute(own, "dp", [(i, (i + by) % dp) for i in range(dp)]) for by in range(1, dp)
    ]
    order = lax.rem(lax.axis_index("dp") - jnp.arange(dp) + dp, dp)
    return jnp.sum(jnp.stack(came)[order], axis=0)


def shape(dims, dtype):
    return jax.ShapeDtypeStruct(dims, dtype)


def levels(ctx):
    chips, found = ctx // 2, []
    while chips > 1:
        width = 4 if chips % 4 == 0 else 2
        chips //= width
        found.append((width, chips, chips))
    return found


def paired(query, key, value, grad, filter_taps):
    length, channels = query.shape
    taps = filter_taps.shape[0]
    ctx = lax.axis_size("ctx")
    share = channels // ctx
    half = channels // 2
    _, one, _, lags = transforms(length, taps)
    block, strip = shape((length, channels), bf16), shape((length, half), bf16)
    spectra = shape((2 * length, half), f32)
    sources = query, grad, key, value
    inside = [(i, i ^ 1) for i in range(ctx)]
    across = [(i, i + 1) for i in range(1, ctx - 1, 2)]
    across += [(i + 1, i) for i, _ in across]

    (urgent,) = call(
        functools.partial(first_kernel, share), "first", sources, [strip],
        far_ins=range(4),
        scratch=[pltpu.VMEM((length, half), bf16)] * 2
        + [pltpu.SemaphoreType.DMA((2, ctx // 2))],
    )
    halo = lax.ppermute(urgent, "ctx", across)
    piece = shape((length, 3 * half // pieces_inside), bf16)
    query, grad, key, value, base, *sends = call(
        functools.partial(prepare_kernel, share), "prepare", (*sources, urgent),
        [block] * 4 + [strip] + [piece] * pieces_inside,
    )
    late = lax.ppermute(base, "ctx", across)
    came = [lax.ppermute(send, "ctx", inside) for send in sends]
    cross, base_spectra = call(
        inside_kernel, "inside", (one, base, *sends, *came), [spectra, spectra]
    )

    def split(level, last):
        width, below, _ = level
        first = shape((below, taps, share), bf16 if last else f32)
        return [first] + [shape((below, taps, share), bf16)] * (width - 1)

    def partner(level, number, over=0):
        step = 2 * level[2] * number
        return [(at, at ^ step ^ over) for at in range(2 * ctx)]

    order = levels(ctx)
    keep, *sends = call(
        functools.partial(lag_kernel, order[0]), "lags",
        (one, lags, halo, cross, base_spectra),
        split(order[0], len(order) == 1),
        scratch=[pltpu.VMEM((ctx // 2, taps, share), f32)],
    )
    held = query, key, value, grad, one, lags
    wide = shape((2, length, channels), bf16)
    inner, *made = call(
        functools.partial(inside_way_kernel, share), "inside_way",
        (*held, filter_taps, *came, keep),
        [wide, shape((2 * length, 4 * length), bf16), block],
        limit=large_bytes,
        flops=3 * 10**9,
    )
    held = *held, *made
    *results, outer = call(
        functools.partial(across_first_kernel, share), "across_first",
        (*held, halo, inner, keep),
        [block] * 4 + [wide],
        far_outs=range(4),
        scratch=[pltpu.SemaphoreType.DMA((2, 4))],
        limit=large_bytes,
        flops=3 * 10**9,
    )
    for level, left in zip(order, order[1:]):
        arrived = [
            lax.ppermute(sends[number - 1], ("dp", "ctx"), partner(level, number))
            for number in (*range(2, level[0]), 1)
        ]
        below = level[1]
        keep, *sends = call(
            functools.partial(join_kernel, left, len(arrived)), "join",
            (keep, *arrived, results[0]),
            split(left, True) + [shape((left[1], taps, share), bf16)],
            far_ins=(len(arrived) + 1,),
            scratch=[pltpu.VMEM((below, taps, share), f32)],
        )
    *sends, twin = sends
    far_parts = [
        lax.ppermute(send, ("dp", "ctx"), partner(order[-1], number, ctx))
        for number, send in enumerate([twin] + sends)
    ]
    parts = [keep] + [
        lax.ppermute(send, ("dp", "ctx"), partner(order[-1], number + 1))
        for number, send in enumerate(sends)
    ]
    parts += far_parts
    *results, _ = call(
        functools.partial(across_late_kernel, share), "across_late",
        (*held, late, keep, *results, outer),
        [block] * 4 + [wide],
        far_ins=range(10, 14),
        far_outs=range(4),
        input_output_aliases={10 + at: at for at in range(5)},
        scratch=[pltpu.SemaphoreType.DMA((half // tile, 2, 2))],
        limit=large_bytes,
    )
    (total,) = call(
        functools.partial(total_kernel, 1.0 / math.sqrt(2 * length * ctx)), "total",
        (*parts, results[0]),
        [shape((taps, share), f32)],
        far_ins=(len(parts),),
        far_outs=(0,),
        scratch=[pltpu.VMEM((taps, share), f32), pltpu.SemaphoreType.DMA],
    )
    return results, total


def plain(query, key, value, grad, filter_taps):
    length, channels = query.shape
    taps = filter_taps.shape[0]
    ctx = lax.axis_size("ctx")
    share = channels // ctx
    first, one, pair, lags = transforms(length, taps)
    block = shape((length, channels), bf16)
    query, grad, key, value, kv, gate = call(
        plain_load_kernel, "load", (query, grad, key, value), [block] * 6,
        far_ins=range(4),
        scratch=[pltpu.SemaphoreType.DMA((4, length // load_rows))],
    )
    before, beyond = shift(kv, "ctx", 1), shift(gate, "ctx", -1)
    (sums,) = call(
        plain_lag_kernel, "lags", (one, pair, lags, before, kv, gate), [shape((taps, channels), bf16)],
    )
    parts = jnp.transpose(sums.reshape(taps, ctx, share), (1, 0, 2))
    pieces = lax.all_to_all(parts, "ctx", 0, 0, tiled=True)
    total = sum_over_dp(jnp.sum(pieces.astype(f32), axis=0))
    total = total * (1.0 / math.sqrt(length * ctx * lax.axis_size("dp")))
    results = call(
        plain_filter_kernel, "filters",
        (first, pair, lags, before, kv, gate, beyond, filter_taps)
        + (query, key, value, grad),
        [block] * 4,
    )
    return results, total


def per_device(query_act, key_act, value_act, grad_out, filter_taps):
    length, channels = query_act.shape[1:]
    ctx, dp = lax.axis_size("ctx"), lax.axis_size("dp")
    share = channels // ctx
    fits = ctx & (ctx - 1) == 0 and ctx > 2 and share % lanes == 0 and tile % share == 0
    fits = fits and filter_taps.shape[0] == length and dp == 2
    run = paired if fits and channels % (2 * tile) == 0 and channels % 1024 == 0 else plain
    results, total = run(query_act[0], key_act[0], value_act[0], grad_out[0], filter_taps)
    return tuple(result[None] for result in results) + (total,)


def solution(mesh):
    sharded = P("dp", "ctx", None)
    return jax.shard_map(
        per_device,
        mesh=mesh,
        in_specs=(sharded, sharded, sharded, sharded, P()),
        out_specs=(sharded, sharded, sharded, sharded, P(None, "ctx")),
        check_vma=False,
    )
```
